32 devices in a mesh: ctx: 8 (over z, y), et: 4 (over x, core).
Axes of the slice: x: 2, y: 2, z: 4, core: 2. Of those that a mesh axis runs over, the one named last changes fastest.
Arguments:
- hidden_in: float32 [1024, 4096], P('ctx', 'et'), may hold values from -60 to 60
- queries: bfloat16 [1024, 4096], P('ctx', 'et'), may hold values from -120 to 120
- keys: bfloat16 [1024, 256], P('ctx'), may hold values from -4.5 to 4.5
- values: bfloat16 [1024, 256], P('ctx'), may hold values from -4 to 4
- out_proj: bfloat16 [4096, 4096], P(None, 'et'), may hold values from -0.5 to 0.5
- norm_gain: float32 [4096], P('et'), may hold values from 0.2 to 2
- expert_ids: int32 [1024, 8], P('ctx'), may hold values from 0 to 127, all different within a row; in each aligned block of 128 rows (0 to 127, 128 to 255, ...) at most 12 rows name the same one
- route_weights: float32 [1024, 8], P('ctx'), may hold values from 0.05 to 1
- w_gate: bfloat16 [8, 4096, 1536], P('ctx', None, 'et'), may hold values from -0.09375 to 0.09375
- w_up: bfloat16 [8, 4096, 1536], P('ctx', None, 'et'), may hold values from -0.09375 to 0.09375
- w_down: bfloat16 [8, 1536, 4096], P('ctx', 'et'), may hold values from -0.15625 to 0.15625
Outputs:
- layer_out: float32 [1024, 4096], P('ctx', 'et')
The draws below stay inside these ranges and needn't reach their ends.
Inputs may be any that keep to these rules, and one draw needn't show every extreme that they name: `expert_ids`: each row names 8 different experts; within the 128 rows of one device no expert is named by more than 12 rows.
All inputs are finite; a program needn't handle non-finite values.
Results may differ from the reference program's by a relative error of at most 0.0025.
Values may be sent and summed in bfloat16 or wider, within the bound.
A program may use at most 64 MiB of HBM per device.

```python
import math
import jax
import jax.numpy as jnp
import numpy as np
from jax import lax

D = 4096
HEADS = 32
KV_HEADS = 2
HD = 128
FF = 1536
ALL_EXPERTS = 128
TOP = 8
TOK_DEV = 128
CAP = 12
EXPERTS = 8
TOKENS = 1024
N_CTX = 8
N_ET = 4


def shared_pair(key):
    normal_keys = jax.random.normal(jax.random.fold_in(key, 1), (TOKENS, KV_HEADS * HD), jnp.float32)
    key_base = jnp.clip(normal_keys, -4.0, 4.0)
    normal_queries = jax.random.normal(jax.random.fold_in(key, 3), (TOKENS, HEADS * HD), jnp.float32)
    query_base = jnp.clip(normal_queries, -4.0, 4.0)
    key_final = key_base
    query_final = query_base
    return (query_final, key_final)


def draw_queries(key, part):
    query_final, key_final = shared_pair(key)
    return query_final.astype(jnp.bfloat16)


def draw_keys(key, part):
    query_final, key_final = shared_pair(key)
    return key_final.astype(jnp.bfloat16)


def draw_hidden_in(key, part):
    key = jax.random.fold_in(key, 31)
    trend = jnp.exp(jnp.linspace(math.log(0.5), math.log(1.5), D)).astype(jnp.float32)
    rough = jnp.exp(jax.random.uniform(jax.random.fold_in(key, 1), (D,), jnp.float32, math.log(0.3), math.log(3.0)))
    row_scale = jnp.exp(jax.random.uniform(jax.random.fold_in(key, 2), (TOKENS, 1), jnp.float32, math.log(0.5), math.log(2.0)))
    entries = jnp.clip(jax.random.normal(jax.random.fold_in(key, 3), (TOKENS, D), jnp.float32), -4.0, 4.0)
    field = entries * row_scale * trend[None, :] * rough[None, :]
    return field.astype(jnp.float32)


def block_levels(stream_key, extent, shards, least, high):
    factor_of, own = 1.0, jax.random.fold_in(stream_key, 6)
    for position, parts in shards:
        steps = jnp.exp(jax.random.uniform(jax.random.fold_in(own, position), (parts,), jnp.float32, least / len(shards), high / len(shards)))
        factor_of = factor_of * jnp.repeat(steps, extent[position] // parts).reshape([-1 if axis == position else 1 for axis in range(len(extent))])
    return factor_of


def deal_out(rng, own, number, rows, count, top, limit, skew):
    order = jax.random.permutation(rng, count)
    packed, ordinary = load_shares(count, rows * top, limit, skew, True), load_shares(count, rows * top, limit, skew, False)
    places = jnp.arange(count)

    def named(sizes, offset_by):
        used = int((sizes > 0).sum())
        fixed = max(1, used // 4)
        moved = fixed + (places - fixed + offset_by * (used - fixed)) % max(1, count - fixed)
        return jnp.zeros((count,), jnp.int32).at[order[jnp.where(places < fixed, places, moved)]].set(jnp.asarray(sizes, jnp.int32))

    sizes = jnp.where(number % 4 == 0, named(packed, number // 4), named(ordinary, number - number // 4 - 1))
    mixed = jax.random.permutation(jax.random.fold_in(own, 3), count)
    donor, receiver = mixed[0:count // 2 * 2:2], mixed[1:count // 2 * 2:2]
    room = jnp.minimum(sizes[donor] - 1, limit - sizes[receiver]) // 2
    room = jnp.where((donor == order[0]) | (receiver == order[0]) | (sizes[receiver] == 0), 0, jnp.maximum(room, 0))
    moved = jax.random.randint(jax.random.fold_in(own, 4), (count // 2,), 0, 1 << 20) % (room + 1)
    sizes = sizes.at[donor].add(-moved).at[receiver].add(moved)
    members = jnp.searchsorted(jnp.cumsum(sizes), jnp.arange(rows * top), side="right").astype(jnp.int32)
    table = members.reshape(top, rows).T
    table = table[jax.random.permutation(jax.random.fold_in(own, 1), rows)]
    offset_by = jax.random.randint(jax.random.fold_in(own, 2), (rows, 1), 0, top)
    return jnp.take_along_axis(table, (jnp.arange(top)[None, :] + offset_by) % top, axis=1)


def load_shares(amount, total, bound, lean, full):
    portions = [(1 << 20) // math.isqrt(standing ** lean) + 1 for standing in range(1, amount + 1)]
    largest = bound if full else min(bound, max(-(-total // amount), total * portions[0] // sum(portions)))
    least = 1 if total - largest >= amount - 1 else 0
    holding, rest = [largest] + [least] * (amount - 1), total - largest - least * (amount - 1)
    while rest > 0:
        free = [i for i in range(1, amount) if holding[i] < largest] or [i for i in range(1, amount) if holding[i] < bound]
        whole, remaining = sum([portions[i] for i in free]), rest
        for i in free:
            more = min(bound - holding[i], max(1, remaining * portions[i] // whole), rest)
            holding[i] = holding[i] + more
            rest = rest - more
    return np.array(holding)


def gaussian(own_key, shape, deviation, limit, shards=(), kind=jnp.bfloat16):
    values = deviation * jax.random.normal(own_key, shape, jnp.float32)
    if shards:
        values = values * block_levels(own_key, shape, shards, -0.22, 0.18)
    return jnp.clip(values, -limit, limit).astype(kind)


def setup_inputs(seed: int = 0) -> dict:
    seeds = jax.random.split(jax.random.key(seed), 12)
    hidden_in = draw_hidden_in(jax.random.fold_in(seeds[11], 71), 0)
    queries = draw_queries(jax.random.fold_in(seeds[11], 71), 0)
    keys = draw_keys(jax.random.fold_in(seeds[11], 71), 0)
    values = gaussian(seeds[3], (TOKENS, KV_HEADS * HD), 1.0, 4.0, ((0, 8),))
    out_proj = gaussian(seeds[4], (HEADS * HD, D), HD ** -0.5, 0.5, ((1, 4),))
    norm_gain = jnp.clip(0.2 + 1.8 * jax.random.uniform(seeds[5], (D,), jnp.float32) ** block_levels(seeds[5], (D,), ((0, 4),), -0.2, 0.2), 0.2, 2.0)
    expert_ids_keys = jax.random.split(jax.random.fold_in(seeds[6], 1), TOKENS // TOK_DEV)
    expert_ids_turns = jax.random.permutation(jax.random.fold_in(seeds[6], 3), TOKENS // TOK_DEV)
    expert_ids = jax.vmap(lambda own, number: deal_out(jax.random.fold_in(seeds[6], 2), own, number, TOK_DEV, ALL_EXPERTS, TOP, CAP, 1))(expert_ids_keys, expert_ids_turns).reshape((TOKENS, TOP))
    route_weights = jnp.clip(jnp.exp(math.log(1.0) - 2.9957323 * jax.random.uniform(seeds[7], (TOKENS, TOP), jnp.float32) ** block_levels(seeds[7], (TOKENS, TOP), ((0, 8),), -0.2, 0.2)), 0.05, 1.0)
    w_gate = gaussian(seeds[8], (EXPERTS, D, FF), D ** -0.5, 0.09375, ((0, 8), (2, 4)))
    w_up = gaussian(seeds[9], (EXPERTS, D, FF), D ** -0.5, 0.09375, ((0, 8), (2, 4)))
    w_down = gaussian(seeds[10], (EXPERTS, FF, D), FF ** -0.5, 0.15625, ((0, 8), (1, 4)))
    return {"hidden_in": hidden_in, "queries": queries, "keys": keys, "values": values, "out_proj": out_proj, "norm_gain": norm_gain, "expert_ids": expert_ids, "route_weights": route_weights, "w_gate": w_gate, "w_up": w_up, "w_down": w_down}


epsilon = 1e-06
masked_score = -1e+30

def reference(hidden_in, queries, keys, values, out_proj, norm_gain, expert_ids, route_weights, w_gate, w_up, w_down):
    tokens = hidden_in.shape[0]
    head_group = HEADS // KV_HEADS
    score_scale = 1.0 / math.sqrt(HD)
    positions = jnp.arange(tokens, dtype=jnp.int32)
    causal = positions[None, :] <= positions[:, None]

    def one_head(head_index):
        query_block = lax.dynamic_slice_in_dim(queries, head_index * HD, HD, 1)
        kv_index = head_index // head_group
        key_block = lax.dynamic_slice_in_dim(keys, kv_index * HD, HD, 1)
        value_block = lax.dynamic_slice_in_dim(values, kv_index * HD, HD, 1)
        scores = jnp.dot(query_block, key_block.T, preferred_element_type=jnp.float32) * score_scale
        scores = jnp.where(causal, scores, masked_score)
        row_max = lax.optimization_barrier(jnp.max(scores, axis=1))
        probs = jnp.where(causal, jnp.exp(scores - row_max[:, None]), 0.0)
        totals = lax.optimization_barrier(jnp.sum(probs, axis=1))
        numer = jnp.dot(probs.astype(jnp.bfloat16), value_block, preferred_element_type=jnp.float32)
        return (numer / totals[:, None]).astype(jnp.bfloat16)
    per_head = lax.map(one_head, jnp.arange(HEADS, dtype=jnp.int32))
    attn = jnp.transpose(per_head, (1, 0, 2)).reshape(tokens, HEADS * HD)
    mixed = hidden_in + jnp.dot(attn, out_proj, preferred_element_type=jnp.float32)
    mean_square = lax.optimization_barrier(jnp.mean(mixed * mixed, axis=1))
    normed = (mixed * lax.rsqrt(mean_square + epsilon)[:, None] * norm_gain[None, :]).astype(jnp.bfloat16)
    padded = jnp.concatenate([normed, jnp.zeros((1, D), jnp.bfloat16)], axis=0)
    slot_rows = N_CTX * CAP
    unit_block = FF // N_ET

    def one_expert(running, expert):
        matches = expert_ids == expert
        weight = lax.optimization_barrier(jnp.sum(jnp.where(matches, route_weights, 0.0), axis=1))
        weight_pad = jnp.concatenate([weight, jnp.zeros((1,), weight.dtype)], axis=0)
        picked = jnp.nonzero(jnp.any(matches, axis=1), size=slot_rows, fill_value=tokens)[0].astype(jnp.int32)
        gathered_rows = padded[picked]
        gate_pre = jnp.dot(gathered_rows, w_gate[expert], preferred_element_type=jnp.float32)
        up_pre = jnp.dot(gathered_rows, w_up[expert], preferred_element_type=jnp.float32)
        activated = (jax.nn.silu(gate_pre) * up_pre).astype(jnp.bfloat16)
        down_whole = w_down[expert]
        expert_sum = jnp.zeros((slot_rows, D), jnp.float32)
        for block_index in range(N_ET):
            block_term = jnp.dot(activated[:, block_index * unit_block:(block_index + 1) * unit_block], down_whole[block_index * unit_block:(block_index + 1) * unit_block], preferred_element_type=jnp.float32)
            expert_sum = expert_sum + lax.optimization_barrier(block_term.astype(jnp.bfloat16)).astype(jnp.float32)
        running = running.at[picked].add(expert_sum * weight_pad[picked][:, None], mode='drop')
        return (running, None)
    routed, _ = lax.scan(one_expert, jnp.zeros((tokens, D), jnp.float32), jnp.arange(EXPERTS, dtype=jnp.int32))
    return mixed + routed
```

```python
import functools
import math

import jax
import jax.numpy as jnp
from jax import lax
from jax.experimental import pallas as pl
from jax.experimental.pallas import tpu as pltpu
from jax.sharding import PartitionSpec as P

D = 4096
HEADS = 32
KV_HEADS = 2
HD = 128
SLOT = 16
EXTRA = 128

epsilon = 1e-06
masked_score = -1e30
BF = jnp.bfloat16
F32 = jnp.float32


def dot(a, b):
    return jnp.dot(a, b, preferred_element_type=F32)


def kernel(
    n, m, AC, NR,
    hidden, queries, keys, values, out_proj, gain, ids, weights, w_gate, w_up, w_down,
    out,
    q_v, kv, wo, wg, wu, wd, hid,
    m_s, acc_s, att, xe, outb, arr, selw, pdown, pin, mine, xs, xin, eo, ret,
    lsem, kv_s, kv_r, kvf_s, kvf_r, att_s, att_r, attf_s,
    d_s, d_r, g_s, g_r, gf_s, p_s, p_r, x_s, x_r, r_s, r_r,
):
    T, F = hidden.shape
    LH = F // HD
    group = HEADS // KV_HEADS
    C = n * SLOT
    U = w_gate.shape[2]
    chips = m // 2
    c = lax.axis_index("ctx")
    j = lax.axis_index("et")
    p = lax.rem(j, 2)
    chip = lax.div(j, 2)
    sib = j + 1 - 2 * p
    kvh = lax.div(j * LH, group)
    head_lanes = pl.ds(pl.multiple_of(kvh * HD, HD), HD)

    def other(o):
        return lax.rem(chip + o, chips)

    def remote(src, dst, ssem, rsem, dc, dj):
        return pltpu.make_async_remote_copy(
            src_ref=src, dst_ref=dst, send_sem=ssem, recv_sem=rsem,
            device_id=(dc, dj), device_id_type=pl.DeviceIdType.MESH,
        )

    def loop(lo, hi, f):
        def step(i, carry):
            f(i)
            return carry
        lax.fori_loop(lo, hi, step, 0)

    local = [
        pltpu.make_async_copy(keys.at[:, head_lanes], kv.at[c, :, pl.ds(0, HD)], lsem.at[0]),
        pltpu.make_async_copy(values.at[:, head_lanes], kv.at[c, :, pl.ds(HD, HD)], lsem.at[1]),
        pltpu.make_async_copy(queries, q_v, lsem.at[2]),
        pltpu.make_async_copy(hidden, hid, lsem.at[3]),
        pltpu.make_async_copy(out_proj, wo, lsem.at[4]),
        pltpu.make_async_copy(w_gate.at[0], wg, lsem.at[5]),
        pltpu.make_async_copy(w_up.at[0], wu, lsem.at[6]),
        pltpu.make_async_copy(w_down.at[0], wd, lsem.at[7]),
    ]
    for copy in local[:3]:
        copy.start()

    barrier = pltpu.get_barrier_semaphore()
    for o in range(1, n):
        pl.semaphore_signal(barrier, inc=1, device_id=(lax.rem(c + o, n), j), device_id_type=pl.DeviceIdType.MESH)
    for o in range(1, m):
        pl.semaphore_signal(barrier, inc=1, device_id=(c, lax.rem(j + o, m)), device_id_type=pl.DeviceIdType.MESH)
    for copy in local[3:]:
        copy.start()
    ones = jnp.ones((T, HD), BF)
    for s in range(n):
        kv[s, :, 2 * HD:] = ones
    local[0].wait()
    local[1].wait()
    pl.semaphore_wait(barrier, n - 1 + m - 1)

    def half(s, which):
        return kv.at[s, :, pl.ds(pl.multiple_of(which * HD, HD), HD)]

    def kv_send(o):
        d = c + o
        @pl.when(d < n)
        def _():
            remote(half(c, p), half(c, p), kv_s.at[o], kv_r.at[c], d, j).start()
    loop(1, n, kv_send)

    col = lax.broadcasted_iota(jnp.int32, (T, C), 1)
    expert_col = lax.div(col, SLOT)
    slot_col = lax.rem(col, SLOT)
    hit = jnp.zeros((T, C), F32)
    weight = jnp.zeros((T, C), F32)
    for k in range(ids.shape[1]):
        same = ids[:, k : k + 1] == expert_col
        hit = hit + jnp.where(same, 1.0, 0.0)
        weight = weight + jnp.where(same, weights[:, k : k + 1], 0.0)
    row_t = lax.broadcasted_iota(jnp.int32, (T, T), 0)
    col_t = lax.broadcasted_iota(jnp.int32, (T, T), 1)
    earlier = jnp.where(col_t < row_t, 1.0, 0.0).astype(BF)
    before = dot(earlier, hit.astype(BF))
    chosen = jnp.where((before == slot_col.astype(F32)) & (hit > 0.5), 1.0, 0.0)
    weight = weight * chosen
    w_hi = weight.astype(BF)
    selw[0] = w_hi
    selw[1] = (weight - w_hi.astype(F32)).astype(BF)
    sel = chosen.T.astype(BF)

    factor = math.log2(math.e) / math.sqrt(HD)
    causal = col_t <= row_t
    local[2].wait()

    def block(s, first):
        k_blk = kv[s, :, :HD]
        v_blk = kv[s, :, HD:]
        for h in range(LH):
            q_h = q_v[:, h * HD : (h + 1) * HD]
            sc = lax.dot_general(q_h, k_blk, (((1,), (1,)), ((), ())), preferred_element_type=F32)
            if first:
                sc = jnp.where(causal, sc, masked_score)
                top = jnp.broadcast_to(jnp.max(sc, axis=1, keepdims=True), (T, HD))
                pr = jnp.where(causal, jnp.exp2((sc - top) * factor), 0.0)
                acc_s[h] = dot(pr.astype(BF), v_blk)
            else:
                old = m_s[h]
                top = jnp.maximum(old, jnp.max(sc, axis=1, keepdims=True))
                pr = jnp.exp2((sc - top) * factor)
                keep = jnp.exp2((old - top) * factor)
                acc_s[h] = acc_s[h] * jnp.concatenate([keep, keep], axis=1) + dot(pr.astype(BF), v_blk)
            m_s[h] = top

    block(c, True)

    def kv_step(o):
        s = c - o
        @pl.when(s >= 0)
        def _():
            remote(half(s, p), half(s, p), kv_s.at[o], kv_r.at[s], c, sib).wait_recv()
            remote(half(s, p), half(s, p), kvf_s.at[s], kvf_r.at[s], c, sib).start()
        prev = s + 1
        @pl.when((prev >= 0) & (o > 1))
        def _():
            remote(half(prev, 1 - p), half(prev, 1 - p), kvf_s.at[prev], kvf_r.at[prev], c, sib).wait_recv()
            block(prev, False)
    loop(1, n + 1, kv_step)

    for h in range(LH):
        att[j, :, h * HD : (h + 1) * HD] = (acc_s[h, :, :HD] / acc_s[h, :, HD:]).astype(BF)
    FC = F // AC

    def piece(jj, k):
        return att.at[jj, :, pl.ds(k * FC, FC)]

    for k in range(AC):
        for o in range(1, chips):
            t = other(o) * 2 + p
            remote(piece(j, k), piece(j, k), att_s.at[t, k], att_r.at[j, k], c, t).start()
        remote(piece(j, k), piece(j, k), att_s.at[sib, k], att_r.at[j, k], c, sib).start()

    local[3].wait()
    local[4].wait()

    def project(jj, k):
        return dot(att[jj, :, k * FC : (k + 1) * FC], wo[pl.ds(pl.multiple_of(jj * F + k * FC, FC), FC), :])

    out[...] = hid[...] + dot(att[j], wo[pl.ds(pl.multiple_of(j * F, F), F), :])
    for k in range(AC):
        remote(piece(sib, k), piece(sib, k), att_s.at[sib, k], att_r.at[sib, k], c, sib).wait_recv()
    if chips == 1:
        out[...] += dot(att[sib], wo[pl.ds(pl.multiple_of(sib * F, F), F), :])
    for o in range(1, chips):
        t = other(o) * 2 + p
        for k in range(AC):
            remote(piece(t, k), piece(t, k), att_s.at[t, k], att_r.at[t, k], c, sib).wait_recv()
            remote(piece(t, k), piece(t, k), attf_s.at[t, k], att_r.at[t, k], c, sib).start()
            if o == 1:
                out[...] += project(sib, k)
        out[...] += dot(att[t], wo[pl.ds(pl.multiple_of(t * F, F), F), :])
    for o in range(1, chips):
        t = other(o) * 2 + 1 - p
        for k in range(AC):
            remote(piece(t, k), piece(t, k), att_s.at[t, k], att_r.at[t, k], c, sib).wait_recv()
        out[...] += dot(att[t], wo[pl.ds(pl.multiple_of(t * F, F), F), :])

    mixed = out[...]
    xe[:, :F] = (mixed * gain[...]).astype(BF)
    squares = jnp.sum(mixed * mixed, axis=1, keepdims=True)
    part0 = squares.astype(BF).astype(F32)
    part1 = (squares - part0).astype(BF).astype(F32)
    part2 = squares - part0 - part1
    lane = lax.broadcasted_iota(jnp.int32, (T, EXTRA), 1)
    xe[:, F:] = jnp.where(
        lane == 0, part0, jnp.where(lane == 1, part1, jnp.where(lane == 2, part2, 0.0))
    ).astype(BF)
    outb[...] = dot(sel, xe[...]).astype(BF).reshape(n, SLOT, F + EXTRA)

    def d_send(o):
        d = lax.rem(c + o, n)
        remote(outb.at[d], arr.at[j, c], d_s.at[o], d_r.at[c], d, j).start()
    loop(1, n, d_send)
    arr[j, c] = outb[c]

    def spread(s):
        for o in range(1, chips):
            t = other(o) * 2 + p
            remote(arr.at[j, s], arr.at[j, s], g_s.at[t, s], g_r.at[j, s], c, t).start()
        remote(arr.at[j, s], arr.at[j, s], g_s.at[sib, s], g_r.at[j, s], c, sib).start()

    def d_step(o):
        s = lax.rem(c + n - o, n)
        @pl.when(o > 0)
        def _():
            remote(outb.at[s], arr.at[j, s], d_s.at[o], d_r.at[s], c, sib).wait_recv()
        spread(s)
    loop(0, n, d_step)

    for i in range(5, 8):
        local[i].wait()

    def rows_of(t):
        return arr[t].reshape(C, F + EXTRA)

    def pre(t):
        x = rows_of(t)
        at = pl.ds(pl.multiple_of(t * F, F), F)
        sq = jnp.sum(x[:, F:].astype(F32), axis=1, keepdims=True)
        return dot(x[:, :F], wg[at, :]), dot(x[:, :F], wu[at, :]), sq

    gate, up, sq = pre(j)

    def add(t, gate, up, sq):
        g1, u1, s1 = pre(t)
        return gate + g1, up + u1, sq + s1

    for o in range(1, chips):
        t = other(o) * 2 + p
        def g_step(i):
            s = lax.rem(c + n - i, n)
            remote(arr.at[t, s], arr.at[t, s], g_s.at[t, s], g_r.at[t, s], c, sib).wait_recv()
            remote(arr.at[t, s], arr.at[t, s], gf_s.at[t, s], g_r.at[t, s], c, sib).start()
        loop(0, n, g_step)

    def g_wait(t):
        def step(s):
            remote(arr.at[t, s], arr.at[t, s], g_s.at[t, s], g_r.at[t, s], c, sib).wait_recv()
        loop(0, n, step)

    g_wait(sib)
    gate, up, sq = add(sib, gate, up, sq)
    for o in range(1, chips):
        gate, up, sq = add(other(o) * 2 + p, gate, up, sq)
    for o in range(1, chips):
        t = other(o) * 2 + 1 - p
        g_wait(t)
        gate, up, sq = add(t, gate, up, sq)
    scale = lax.rsqrt(sq / D + epsilon)
    gate = gate * scale
    up = up * scale
    act = (gate / (1.0 + jnp.exp(-gate)) * up).astype(BF)

    CR = C // NR
    NC = n // NR

    def down(t, r):
        return dot(act[r * CR : (r + 1) * CR], wd[:, pl.ds(pl.multiple_of(t * F, F), F)])

    def at_rows(r):
        return pl.ds(r * CR, CR)

    def pair(r, q):
        return remote(pdown.at[q, at_rows(r)], pin.at[q, at_rows(r)], p_s.at[q, r], p_r.at[q, r], c, sib)

    def cross(r, o):
        q = other(o)
        return remote(xs.at[q, at_rows(r)], xin.at[chip, at_rows(r)], x_s.at[q, r], x_r.at[chip, r], c, q * 2 + p)

    for r in range(NR):
        for o in list(range(1, chips)) + [0]:
            q = other(o)
            pdown[q, r * CR : (r + 1) * CR] = down(q * 2 + 1 - p, r).astype(BF)
            pair(r, q).start()
    for r in range(NR):
        rr = slice(r * CR, (r + 1) * CR)
        for o in range(1, chips):
            q = other(o)
            part = down(q * 2 + p, r).astype(BF).astype(F32)
            pair(r, q).wait_recv()
            xs[q, rr] = (part + pin[q, rr].astype(F32)).astype(BF)
            cross(r, o).start()
    for r in range(NR):
        rr = slice(r * CR, (r + 1) * CR)
        mine[rr] = down(chip * 2 + p, r).astype(BF).astype(F32)
        pair(r, chip).wait_recv()
        mine[rr] += pin[chip, rr].astype(F32)
    for r in range(NR):
        rr = slice(r * CR, (r + 1) * CR)
        total = mine[rr]
        for o in range(1, chips):
            q = other(o)
            remote(xin.at[q, at_rows(r)], xin.at[q, at_rows(r)], x_s.at[q, r], x_r.at[q, r], c, sib).wait_recv()
            total = total + xin[q, rr].astype(F32)
        eo[r * NC : (r + 1) * NC] = total.astype(BF).reshape(NC, SLOT, F)

        def r_send(s):
            @pl.when(s != c)
            def _():
                remote(eo.at[s], ret.at[c], r_s.at[s], r_r.at[c], s, j).start()
            @pl.when(s == c)
            def _():
                ret[c] = eo[c]
        loop(r * NC, (r + 1) * NC, r_send)

    def r_wait(s):
        @pl.when(s != c)
        def _():
            remote(eo.at[s], ret.at[s], r_s.at[s], r_r.at[s], s, j).wait_recv()
    loop(0, n, r_wait)
    back = ret[...].reshape(C, F)
    out[...] += dot(selw[0], back) + dot(selw[1], back)

    def kv_done(o):
        @pl.when(c + o < n)
        def _():
            remote(half(c, p), half(c, p), kv_s.at[o], kv_r.at[c], c, sib).wait_send()
        @pl.when(c - o >= 0)
        def _():
            s = c - o
            remote(half(s, p), half(s, p), kvf_s.at[s], kvf_r.at[s], c, sib).wait_send()
        remote(outb.at[o], arr.at[j, c], d_s.at[o], d_r.at[c], c, sib).wait_send()
    loop(1, n, kv_done)

    def rest_done(s):
        for o in range(1, chips):
            t = other(o) * 2 + p
            remote(arr.at[j, s], arr.at[j, s], g_s.at[t, s], g_r.at[j, s], c, t).wait_send()
            remote(arr.at[t, s], arr.at[t, s], gf_s.at[t, s], g_r.at[t, s], c, sib).wait_send()
        remote(arr.at[j, s], arr.at[j, s], g_s.at[sib, s], g_r.at[j, s], c, sib).wait_send()
        @pl.when(s != c)
        def _():
            remote(eo.at[s], ret.at[c], r_s.at[s], r_r.at[c], s, j).wait_send()
    loop(0, n, rest_done)
    for k in range(AC):
        for o in range(1, chips):
            t = other(o) * 2 + p
            remote(piece(j, k), piece(j, k), att_s.at[t, k], att_r.at[j, k], c, t).wait_send()
            remote(piece(t, k), piece(t, k), attf_s.at[t, k], att_r.at[t, k], c, sib).wait_send()
        remote(piece(j, k), piece(j, k), att_s.at[sib, k], att_r.at[j, k], c, sib).wait_send()
    for r in range(NR):
        for o in range(chips):
            pair(r, other(o)).wait_send()
        for o in range(1, chips):
            cross(r, o).wait_send()


def body(hidden, queries, keys, values, out_proj, gain, ids, weights, w_gate, w_up, w_down):
    n = lax.axis_size("ctx")
    m = lax.axis_size("et")
    T, F = hidden.shape
    U = w_gate.shape[2]
    LH = F // HD
    C = n * SLOT
    chips = m // 2
    AC = 4 if F % 512 == 0 else 2
    NR = 2
    DMA = pltpu.SemaphoreType.DMA
    V = pltpu.VMEM
    any_ = pl.BlockSpec(memory_space=pl.ANY)
    vm = pl.BlockSpec(memory_space=pltpu.VMEM)
    return pl.pallas_call(
        functools.partial(kernel, n, m, AC, NR),
        out_shape=jax.ShapeDtypeStruct((T, F), F32),
        in_specs=[any_, any_, any_, any_, any_, vm, vm, vm, any_, any_, any_],
        out_specs=vm,
        scratch_shapes=[
            V((T, F), BF),
            V((n, T, 3 * HD), BF),
            V(out_proj.shape, BF),
            V(w_gate.shape[1:], BF),
            V(w_up.shape[1:], BF),
            V(w_down.shape[1:], BF),
            V((T, F), F32),
            V((LH, T, HD), F32),
            V((LH, T, 2 * HD), F32),
            V((m, T, F), BF),
            V((T, F + EXTRA), BF),
            V((n, SLOT, F + EXTRA), BF),
            V((m, n, SLOT, F + EXTRA), BF),
            V((2, T, C), BF),
            V((chips, C, F), BF),
            V((chips, C, F), BF),
            V((C, F), F32),
            V((chips, C, F), BF),
            V((chips, C, F), BF),
            V((n, SLOT, F), BF),
            V((n, SLOT, F), BF),
            DMA((8,)),
            DMA((n,)), DMA((n,)), DMA((n,)), DMA((n,)),
            DMA((m, AC)), DMA((m, AC)), DMA((m, AC)),
            DMA((n,)), DMA((n,)),
            DMA((m, n)), DMA((m, n)), DMA((m, n)),
            DMA((chips, NR)), DMA((chips, NR)),
            DMA((chips, NR)), DMA((chips, NR)),
            DMA((n,)), DMA((n,)),
        ],
        compiler_params=pltpu.CompilerParams(
            collective_id=0, has_side_effects=True, vmem_limit_bytes=58 * 1024 * 1024
        ),
        cost_estimate=pl.CostEstimate(flops=4 * 10**9, bytes_accessed=2 * 10**7, transcendentals=10**6),
    )(
        hidden, queries, keys, values, out_proj, gain.reshape(1, F), ids, weights,
        w_gate, w_up, w_down,
    )


def solution(mesh):
    return jax.shard_map(
        body,
        mesh=mesh,
        in_specs=(
            P("ctx", "et"),
            P("ctx", "et"),
            P("ctx", None),
            P("ctx", None),
            P(None, "et"),
            P("et"),
            P("ctx", None),
            P("ctx", None),
            P("ctx", None, "et"),
            P("ctx", None, "et"),
            P("ctx", "et", None),
        ),
        out_specs=P("ctx", "et"),
        check_vma=False,
    )
```

```python
import functools
import math

import jax
import jax.numpy as jnp
from jax import lax
from jax.experimental import pallas as pl
from jax.experimental.pallas import tpu as pltpu
from jax.sharding import PartitionSpec as P

D = 4096
HEADS = 32
KV_HEADS = 2
HD = 128
SLOT = 16
EXTRA = 128

epsilon = 1e-06
masked_score = -1e30
BF = jnp.bfloat16
F32 = jnp.float32


def dot(a, b):
    return jnp.dot(a, b, preferred_element_type=F32)


def kernel(
    n, m, AC, NR,
    hidden, queries, keys, values, out_proj, gain, ids, weights, w_gate, w_up, w_down,
    out,
    q_v, kv, q_t, wo, wg, wu, wd, hid,
    m_s, l_s, acc_s, att, xe, outb, arr, selw, pdown, pin, mine, xs, xin, eo, ret,
    lsem, kv_s, kv_r, kvf_s, kvf_r, att_s, att_r, attf_s,
    d_s, d_r, g_s, g_r, gf_s, p_s, p_r, x_s, x_r, r_s, r_r,
):
    T, F = hidden.shape
    LH = F // HD
    group = HEADS // KV_HEADS
    C = n * SLOT
    U = w_gate.shape[2]
    chips = m // 2
    c = lax.axis_index("ctx")
    j = lax.axis_index("et")
    p = lax.rem(j, 2)
    chip = lax.div(j, 2)
    sib = j + 1 - 2 * p
    kvh = lax.div(j * LH, group)
    head_lanes = pl.ds(pl.multiple_of(kvh * HD, HD), HD)

    def other(o):
        return lax.rem(chip + o, chips)

    def remote(src, dst, ssem, rsem, dc, dj):
        return pltpu.make_async_remote_copy(
            src_ref=src, dst_ref=dst, send_sem=ssem, recv_sem=rsem,
            device_id=(dc, dj), device_id_type=pl.DeviceIdType.MESH,
        )

    def loop(lo, hi, f):
        def step(i, carry):
            f(i)
            return carry
        lax.fori_loop(lo, hi, step, 0)

    def kv_sent():
        def step(o):
            @pl.when(c + o < n)
            def _():
                remote(half(c, p), half(c, p), kv_s.at[o], kv_r.at[c], c, sib).wait_send()
            @pl.when(c - o >= 0)
            def _():
                s = c - o
                remote(half(s, p), half(s, p), kvf_s.at[s], kvf_r.at[s], c, sib).wait_send()
        loop(1, n, step)

    def att_sent():
        for k in range(AC):
            for o in range(1, chips):
                t = other(o) * 2 + p
                remote(piece(j, k), piece(j, k), att_s.at[t, k], att_r.at[j, k], c, t).wait_send()
                remote(piece(t, k), piece(t, k), attf_s.at[t, k], att_r.at[t, k], c, sib).wait_send()
            remote(piece(j, k), piece(j, k), att_s.at[sib, k], att_r.at[j, k], c, sib).wait_send()

    def rows_sent():
        def step(s):
            @pl.when(s > 0)
            def _():
                remote(outb.at[s], arr.at[j, c], d_s.at[s], d_r.at[c], c, sib).wait_send()
            for o in range(1, chips):
                t = other(o) * 2 + p
                remote(arr.at[j, s], arr.at[j, s], g_s.at[t, s], g_r.at[j, s], c, t).wait_send()
                remote(arr.at[t, s], arr.at[t, s], gf_s.at[t, s], g_r.at[t, s], c, sib).wait_send()
            remote(arr.at[j, s], arr.at[j, s], g_s.at[sib, s], g_r.at[j, s], c, sib).wait_send()
        loop(0, n, step)

    def rest_sent():
        for r in range(NR):
            for o in range(chips):
                pair(r, other(o)).wait_send()
            for o in range(1, chips):
                cross(r, o).wait_send()
        def step(s):
            @pl.when(s != c)
            def _():
                remote(eo.at[s], ret.at[c], r_s.at[s], r_r.at[c], s, j).wait_send()
        loop(0, n, step)

    local = [
        pltpu.make_async_copy(keys.at[:, head_lanes], kv.at[c, :, pl.ds(0, HD)], lsem.at[0]),
        pltpu.make_async_copy(values.at[:, head_lanes], kv.at[c, :, pl.ds(HD, HD)], lsem.at[1]),
        pltpu.make_async_copy(queries, q_v, lsem.at[2]),
        pltpu.make_async_copy(hidden, hid, lsem.at[3]),
        pltpu.make_async_copy(out_proj, wo, lsem.at[4]),
        pltpu.make_async_copy(w_gate.at[0], wg, lsem.at[5]),
        pltpu.make_async_copy(w_up.at[0], wu, lsem.at[6]),
        pltpu.make_async_copy(w_down.at[0], wd, lsem.at[7]),
    ]
    for copy in local[:3]:
        copy.start()

    barrier = pltpu.get_barrier_semaphore()
    for o in range(1, n):
        pl.semaphore_signal(barrier, inc=1, device_id=(lax.rem(c + o, n), j), device_id_type=pl.DeviceIdType.MESH)
    for o in range(1, m):
        pl.semaphore_signal(barrier, inc=1, device_id=(c, lax.rem(j + o, m)), device_id_type=pl.DeviceIdType.MESH)
    for copy in local[3:]:
        copy.start()
    local[0].wait()
    local[1].wait()
    pl.semaphore_wait(barrier, n - 1 + m - 1)

    def half(s, which):
        return kv.at[s, :, pl.ds(pl.multiple_of(which * HD, HD), HD)]

    def kv_send(o):
        d = c + o
        @pl.when(d < n)
        def _():
            remote(half(c, p), half(c, p), kv_s.at[o], kv_r.at[c], d, j).start()
    loop(1, n, kv_send)

    slot_row = lax.broadcasted_iota(jnp.int32, (C, T), 0)
    expert_row = lax.div(slot_row, SLOT)
    place = lax.rem(slot_row, SLOT).astype(F32)
    hit = jnp.zeros((C, T), F32)
    weight = jnp.zeros((C, T), F32)
    for k in range(ids.shape[0]):
        same = ids[k : k + 1, :] == expert_row
        hit = hit + jnp.where(same, 1.0, 0.0)
        weight = weight + jnp.where(same, weights[k : k + 1, :], 0.0)
    row_t = lax.broadcasted_iota(jnp.int32, (T, T), 0)
    col_t = lax.broadcasted_iota(jnp.int32, (T, T), 1)
    earlier = jnp.where(row_t < col_t, 1.0, 0.0).astype(BF)
    before = dot(hit.astype(BF), earlier)
    chosen = jnp.where((before == place) & (hit > 0.5), 1.0, 0.0)
    weight = (weight * chosen).T
    w_hi = weight.astype(BF)
    selw[0] = w_hi
    selw[1] = (weight - w_hi.astype(F32)).astype(BF)
    sel = chosen.astype(BF)

    factor = math.log2(math.e) / math.sqrt(HD)
    W = min(256, LH * T)
    causal = jnp.concatenate([row_t <= col_t] * (W // T), axis=1)
    local[2].wait()
    for h in range(LH):
        q_t[:, h * T : (h + 1) * T] = q_v[:, h * HD : (h + 1) * HD].T

    def block(k_blk, v_blk, first):
        v_t = v_blk.T
        for w in range(LH * T // W):
            at = slice(w * W, (w + 1) * W)
            sc = dot(k_blk, q_t[:, at])
            if first:
                sc = jnp.where(causal, sc, masked_score)
                top = jnp.max(sc, axis=0, keepdims=True)
                pr = jnp.where(causal, jnp.exp2((sc - top) * factor), 0.0)
                l_s[:, at] = jnp.sum(pr, axis=0, keepdims=True)
                acc_s[:, at] = dot(v_t, pr.astype(BF))
            else:
                old = m_s[:, at]
                top = jnp.maximum(old, jnp.max(sc, axis=0, keepdims=True))
                pr = jnp.exp2((sc - top) * factor)
                keep = jnp.exp2((old - top) * factor)
                l_s[:, at] = l_s[:, at] * keep + jnp.sum(pr, axis=0, keepdims=True)
                acc_s[:, at] = acc_s[:, at] * keep + dot(v_t, pr.astype(BF))
            m_s[:, at] = top

    block(kv[c, :, :HD], kv[c, :, HD:], True)

    def kv_step(i):
        for o in (2 * i - 1, 2 * i):
            s = c - o
            @pl.when(s >= 0)
            def _():
                remote(half(s, p), half(s, p), kv_s.at[0], kv_r.at[s], c, sib).wait_recv()
                remote(half(s, p), half(s, p), kvf_s.at[s], kvf_r.at[s], c, sib).start()
        hi = c - (2 * i - 3)
        lo = hi - 1
        def arrived(s):
            remote(half(s, 1 - p), half(s, 1 - p), kvf_s.at[s], kvf_r.at[s], c, sib).wait_recv()
        @pl.when((i > 1) & (lo >= 0))
        def _():
            arrived(hi)
            arrived(lo)
            both = kv[pl.ds(lo, 2)].reshape(2 * T, 2 * HD)
            block(both[:, :HD], both[:, HD:], False)
        @pl.when((i > 1) & (lo == -1))
        def _():
            arrived(hi)
            block(kv[hi, :, :HD], kv[hi, :, HD:], False)
    loop(1, n // 2 + 2, kv_step)

    for h in range(LH):
        at = slice(h * T, (h + 1) * T)
        att[j, :, h * HD : (h + 1) * HD] = (acc_s[:, at] / l_s[:, at]).T.astype(BF)
    FC = F // AC

    def piece(jj, k):
        return att.at[jj, :, pl.ds(k * FC, FC)]

    for k in range(AC):
        for o in range(1, chips):
            t = other(o) * 2 + p
            remote(piece(j, k), piece(j, k), att_s.at[t, k], att_r.at[j, k], c, t).start()
        remote(piece(j, k), piece(j, k), att_s.at[sib, k], att_r.at[j, k], c, sib).start()

    local[3].wait()
    local[4].wait()

    def project(jj, k):
        return dot(att[jj, :, k * FC : (k + 1) * FC], wo[pl.ds(pl.multiple_of(jj * F + k * FC, FC), FC), :])

    out[...] = hid[...] + dot(att[j], wo[pl.ds(pl.multiple_of(j * F, F), F), :])
    for k in range(AC):
        remote(piece(sib, k), piece(sib, k), att_s.at[sib, k], att_r.at[sib, k], c, sib).wait_recv()
    if chips == 1:
        out[...] += dot(att[sib], wo[pl.ds(pl.multiple_of(sib * F, F), F), :])
    for o in range(1, chips):
        t = other(o) * 2 + p
        for k in range(AC):
            remote(piece(t, k), piece(t, k), att_s.at[t, k], att_r.at[t, k], c, sib).wait_recv()
            remote(piece(t, k), piece(t, k), attf_s.at[t, k], att_r.at[t, k], c, sib).start()
            if o == 1:
                out[...] += project(sib, k)
        out[...] += dot(att[t], wo[pl.ds(pl.multiple_of(t * F, F), F), :])
    for o in range(1, chips):
        t = other(o) * 2 + 1 - p
        for k in range(AC):
            remote(piece(t, k), piece(t, k), att_s.at[t, k], att_r.at[t, k], c, sib).wait_recv()
        out[...] += dot(att[t], wo[pl.ds(pl.multiple_of(t * F, F), F), :])

    mixed = out[...]
    xe[:, :F] = (mixed * gain[...]).astype(BF)
    squares = jnp.sum(mixed * mixed, axis=1, keepdims=True)
    part0 = squares.astype(BF).astype(F32)
    part1 = (squares - part0).astype(BF).astype(F32)
    part2 = squares - part0 - part1
    lane = lax.broadcasted_iota(jnp.int32, (T, EXTRA), 1)
    xe[:, F:] = jnp.where(
        lane == 0, part0, jnp.where(lane == 1, part1, jnp.where(lane == 2, part2, 0.0))
    ).astype(BF)
    outb[...] = dot(sel, xe[...]).astype(BF).reshape(n, SLOT, F + EXTRA)

    def d_send(o):
        d = lax.rem(c + o, n)
        remote(outb.at[d], arr.at[j, c], d_s.at[o], d_r.at[c], d, j).start()
    loop(1, n, d_send)
    arr[j, c] = outb[c]

    def spread(s):
        for o in range(1, chips):
            t = other(o) * 2 + p
            remote(arr.at[j, s], arr.at[j, s], g_s.at[t, s], g_r.at[j, s], c, t).start()
        remote(arr.at[j, s], arr.at[j, s], g_s.at[sib, s], g_r.at[j, s], c, sib).start()

    def d_step(o):
        s = lax.rem(c + n - o, n)
        @pl.when(o > 0)
        def _():
            remote(outb.at[s], arr.at[j, s], d_s.at[o], d_r.at[s], c, sib).wait_recv()
        spread(s)
    loop(0, n, d_step)

    for i in range(5, 8):
        local[i].wait()

    def rows_of(t):
        return arr[t].reshape(C, F + EXTRA)

    def pre(t):
        x = rows_of(t)
        at = pl.ds(pl.multiple_of(t * F, F), F)
        sq = jnp.sum(x[:, F:].astype(F32), axis=1, keepdims=True)
        return dot(x[:, :F], wg[at, :]), dot(x[:, :F], wu[at, :]), sq

    gate, up, sq = pre(j)

    def add(t, gate, up, sq):
        g1, u1, s1 = pre(t)
        return gate + g1, up + u1, sq + s1

    for o in range(1, chips):
        t = other(o) * 2 + p
        def g_step(i):
            s = lax.rem(c + n - i, n)
            remote(arr.at[t, s], arr.at[t, s], g_s.at[t, s], g_r.at[t, s], c, sib).wait_recv()
            remote(arr.at[t, s], arr.at[t, s], gf_s.at[t, s], g_r.at[t, s], c, sib).start()
        loop(0, n, g_step)

    def g_wait(t):
        def step(s):
            remote(arr.at[t, s], arr.at[t, s], g_s.at[t, s], g_r.at[t, s], c, sib).wait_recv()
        loop(0, n, step)

    g_wait(sib)
    gate, up, sq = add(sib, gate, up, sq)
    for o in range(1, chips):
        gate, up, sq = add(other(o) * 2 + p, gate, up, sq)
    for o in range(1, chips):
        t = other(o) * 2 + 1 - p
        g_wait(t)
        gate, up, sq = add(t, gate, up, sq)
    scale = lax.rsqrt(sq / D + epsilon)
    gate = gate * scale
    up = up * scale
    act = (gate / (1.0 + jnp.exp(-gate)) * up).astype(BF)

    CR = C // NR
    NC = n // NR

    def down(t, r):
        return dot(act[r * CR : (r + 1) * CR], wd[:, pl.ds(pl.multiple_of(t * F, F), F)])

    def at_rows(r):
        return pl.ds(r * CR, CR)

    def pair(r, q):
        return remote(pdown.at[q, at_rows(r)], pin.at[q, at_rows(r)], p_s.at[q, r], p_r.at[q, r], c, sib)

    def cross(r, o):
        q = other(o)
        return remote(xs.at[q, at_rows(r)], xin.at[chip, at_rows(r)], x_s.at[q, r], x_r.at[chip, r], c, q * 2 + p)

    for r in range(NR):
        for o in list(range(1, chips)) + [0]:
            q = other(o)
            pdown[q, r * CR : (r + 1) * CR] = down(q * 2 + 1 - p, r).astype(BF)
            pair(r, q).start()
    for r in range(NR):
        rr = slice(r * CR, (r + 1) * CR)
        for o in range(1, chips):
            q = other(o)
            part = down(q * 2 + p, r).astype(BF).astype(F32)
            pair(r, q).wait_recv()
            xs[q, rr] = (part + pin[q, rr].astype(F32)).astype(BF)
            cross(r, o).start()
    for r in range(NR):
        rr = slice(r * CR, (r + 1) * CR)
        mine[rr] = down(chip * 2 + p, r).astype(BF).astype(F32)
        pair(r, chip).wait_recv()
        mine[rr] += pin[chip, rr].astype(F32)
    for r in range(NR):
        rr = slice(r * CR, (r + 1) * CR)
        total = mine[rr]
        for o in range(1, chips):
            q = other(o)
            remote(xin.at[q, at_rows(r)], xin.at[q, at_rows(r)], x_s.at[q, r], x_r.at[q, r], c, sib).wait_recv()
            total = total + xin[q, rr].astype(F32)
        eo[r * NC : (r + 1) * NC] = total.astype(BF).reshape(NC, SLOT, F)

        def r_send(s):
            @pl.when(s != c)
            def _():
                remote(eo.at[s], ret.at[c], r_s.at[s], r_r.at[c], s, j).start()
            @pl.when(s == c)
            def _():
                ret[c] = eo[c]
        loop(r * NC, (r + 1) * NC, r_send)

    def r_wait(s):
        @pl.when(s != c)
        def _():
            remote(eo.at[s], ret.at[s], r_s.at[s], r_r.at[s], s, j).wait_recv()
    loop(0, n, r_wait)
    back = ret[...].reshape(C, F)
    out[...] += dot(selw[0], back) + dot(selw[1], back)

    kv_sent()
    att_sent()
    rows_sent()
    rest_sent()


def body(hidden, queries, keys, values, out_proj, gain, ids, weights, w_gate, w_up, w_down):
    n = lax.axis_size("ctx")
    m = lax.axis_size("et")
    T, F = hidden.shape
    U = w_gate.shape[2]
    LH = F // HD
    C = n * SLOT
    chips = m // 2
    AC = 4 if F % 512 == 0 else 2
    NR = 2
    DMA = pltpu.SemaphoreType.DMA
    V = pltpu.VMEM
    any_ = pl.BlockSpec(memory_space=pl.ANY)
    vm = pl.BlockSpec(memory_space=pltpu.VMEM)
    return pl.pallas_call(
        functools.partial(kernel, n, m, AC, NR),
        out_shape=jax.ShapeDtypeStruct((T, F), F32),
        in_specs=[any_, any_, any_, any_, any_, vm, vm, vm, any_, any_, any_],
        out_specs=vm,
        scratch_shapes=[
            V((T, F), BF),
            V((n, T, 2 * HD), BF),
            V((HD, LH * T), BF),
            V(out_proj.shape, BF),
            V(w_gate.shape[1:], BF),
            V(w_up.shape[1:], BF),
            V(w_down.shape[1:], BF),
            V((T, F), F32),
            V((1, LH * T), F32),
            V((1, LH * T), F32),
            V((HD, LH * T), F32),
            V((m, T, F), BF),
            V((T, F + EXTRA), BF),
            V((n, SLOT, F + EXTRA), BF),
            V((m, n, SLOT, F + EXTRA), BF),
            V((2, T, C), BF),
            V((chips, C, F), BF),
            V((chips, C, F), BF),
            V((C, F), F32),
            V((chips, C, F), BF),
            V((chips, C, F), BF),
            V((n, SLOT, F), BF),
            V((n, SLOT, F), BF),
            DMA((8,)),
            DMA((n,)), DMA((n,)), DMA((n,)), DMA((n,)),
            DMA((m, AC)), DMA((m, AC)), DMA((m, AC)),
            DMA((n,)), DMA((n,)),
            DMA((m, n)), DMA((m, n)), DMA((m, n)),
            DMA((chips, NR)), DMA((chips, NR)),
            DMA((chips, NR)), DMA((chips, NR)),
            DMA((n,)), DMA((n,)),
        ],
        compiler_params=pltpu.CompilerParams(
            collective_id=0, has_side_effects=True, vmem_limit_bytes=58 * 1024 * 1024
        ),
        cost_estimate=pl.CostEstimate(flops=4 * 10**9, bytes_accessed=2 * 10**7, transcendentals=10**6),
    )(
        hidden, queries, keys, values, out_proj, gain.reshape(1, F), ids.T, weights.T,
        w_gate, w_up, w_down,
    )


def solution(mesh):
    return jax.shard_map(
        body,
        mesh=mesh,
        in_specs=(
            P("ctx", "et"),
            P("ctx", "et"),
            P("ctx", None),
            P("ctx", None),
            P(None, "et"),
            P("et"),
            P("ctx", None),
            P("ctx", None),
            P("ctx", None, "et"),
            P("ctx", None, "et"),
            P("ctx", "et", None),
        ),
        out_specs=P("ctx", "et"),
        check_vma=False,
    )
```

```python
import functools
import math

import jax
import jax.numpy as jnp
from jax import lax
from jax.experimental import pallas as pl
from jax.experimental.pallas import tpu as pltpu
from jax.sharding import PartitionSpec as P

D = 4096
HEADS = 32
KV_HEADS = 2
HD = 128
CAP = 12
SLOT = 16
EXTRA = 128

epsilon = 1e-06
masked_score = -1e30
BF = jnp.bfloat16
F32 = jnp.float32


def dot(a, b):
    return jnp.dot(a, b, preferred_element_type=F32)


def kernel(
    n, m, AC, NR, G, LAGS,
    hidden, queries, keys, values, out_proj, gain, ids, weights, w_gate, w_up, w_down,
    out,
    q_v, kv, q_t, wo, wg, wu, wd, hid,
    m_s, l_s, acc_s, att, xe, outb, arr, selw, pdown, pin, mine, xs, xin, eo, ret,
    lsem, kv_s, kv_r, kvf_s, kvf_r, att_s, att_r, attf_s,
    d_s, d_r, g_s, g_r, gf_s, p_s, p_r, x_s, x_r, r_s, r_r,
):
    T, F = hidden.shape
    LH = F // HD
    group = HEADS // KV_HEADS
    C = n * SLOT
    U = w_gate.shape[2]
    chips = m // 2
    NG = n // G
    FP = arr.shape[3] - EXTRA
    FQ = F - FP
    groups = FP // FQ if FQ else 0
    c = lax.axis_index("ctx")
    j = lax.axis_index("et")
    p = lax.rem(j, 2)
    chip = lax.div(j, 2)
    sib = j + 1 - 2 * p
    kvh = lax.div(j * LH, group)
    head_lanes = pl.ds(pl.multiple_of(kvh * HD, HD), HD)

    def other(o):
        return lax.rem(chip + o, chips)

    def remote(src, dst, ssem, rsem, dc, dj):
        return pltpu.make_async_remote_copy(
            src_ref=src, dst_ref=dst, send_sem=ssem, recv_sem=rsem,
            device_id=(dc, dj), device_id_type=pl.DeviceIdType.MESH,
        )

    def loop(lo, hi, f):
        def step(i, carry):
            f(i)
            return carry
        lax.fori_loop(lo, hi, step, 0)

    def kv_sent():
        def step(o):
            @pl.when(c + o < n)
            def _():
                remote(half(c, p), half(c, p), kv_s.at[o], kv_r.at[c], c, sib).wait_send()
            @pl.when(c - o >= 0)
            def _():
                s = c - o
                remote(half(s, p), half(s, p), kvf_s.at[s], kvf_r.at[s], c, sib).wait_send()
        loop(1, n, step)

    def att_sent():
        for k in range(AC):
            for o in range(1, chips):
                t = other(o) * 2 + p
                remote(piece(j, k), piece(j, k), att_s.at[t, k], att_r.at[j, k], c, t).wait_send()
                remote(piece(t, k), piece(t, k), attf_s.at[t, k], att_r.at[t, k], c, sib).wait_send()
            remote(piece(j, k), piece(j, k), att_s.at[sib, k], att_r.at[j, k], c, sib).wait_send()

    def rows_sent():
        def step(s):
            remote(outb.at[s], arr.at[j, c], d_s.at[s], d_r.at[c], c, sib).wait_send()
        loop(1, n, step)

        def step_group(i):
            for o in range(1, chips):
                t = other(o) * 2 + p
                remote(rows(j, i), rows(j, i), g_s.at[t, i], g_r.at[j, i], c, t).wait_send()
                remote(rows(t, i), rows(t, i), gf_s.at[t, i], g_r.at[t, i], c, sib).wait_send()
            remote(rows(j, i), rows(j, i), g_s.at[sib, i], g_r.at[j, i], c, sib).wait_send()
        loop(0, NG, step_group)

    def rest_sent():
        for r in range(NR):
            for o in range(chips):
                pair(r, other(o)).wait_send()
            for o in range(1, chips):
                cross(r, o).wait_send()
        def step(s):
            @pl.when(s != c)
            def _():
                remote(eo.at[s], ret.at[c], r_s.at[s], r_r.at[c], s, j).wait_send()
        loop(0, n, step)

    local = [
        pltpu.make_async_copy(keys.at[:, head_lanes], kv.at[c, :, pl.ds(0, HD)], lsem.at[0]),
        pltpu.make_async_copy(values.at[:, head_lanes], kv.at[c, :, pl.ds(HD, HD)], lsem.at[1]),
        pltpu.make_async_copy(queries, q_v, lsem.at[2]),
        pltpu.make_async_copy(hidden, hid, lsem.at[3]),
        pltpu.make_async_copy(out_proj, wo, lsem.at[4]),
        pltpu.make_async_copy(w_gate.at[0], wg, lsem.at[5]),
        pltpu.make_async_copy(w_up.at[0], wu, lsem.at[6]),
        pltpu.make_async_copy(w_down.at[0], wd, lsem.at[7]),
    ]
    for copy in local[:3]:
        copy.start()

    barrier = pltpu.get_barrier_semaphore()
    for o in range(1, n):
        pl.semaphore_signal(barrier, inc=1, device_id=(lax.rem(c + o, n), j), device_id_type=pl.DeviceIdType.MESH)
    for o in range(1, m):
        pl.semaphore_signal(barrier, inc=1, device_id=(c, lax.rem(j + o, m)), device_id_type=pl.DeviceIdType.MESH)
    local[0].wait()
    local[1].wait()
    pl.semaphore_wait(barrier, n - 1 + m - 1)

    def half(s, which):
        return kv.at[s, :, pl.ds(pl.multiple_of(which * HD, HD), HD)]

    def kv_send(o):
        d = c + o
        @pl.when(d < n)
        def _():
            remote(half(c, p), half(c, p), kv_s.at[o], kv_r.at[c], d, j).start()
    loop(1, n, kv_send)
    for copy in local[3:5]:
        copy.start()

    slot_row = lax.broadcasted_iota(jnp.int32, (C, T), 0)
    expert_row = lax.div(slot_row, SLOT)
    place = lax.rem(slot_row, SLOT).astype(F32)
    hit = jnp.zeros((C, T), F32)
    weight = jnp.zeros((C, T), F32)
    for k in range(ids.shape[0]):
        same = ids[k : k + 1, :] == expert_row
        hit = hit + jnp.where(same, 1.0, 0.0)
        weight = weight + jnp.where(same, weights[k : k + 1, :], 0.0)
    row_t = lax.broadcasted_iota(jnp.int32, (T, T), 0)
    col_t = lax.broadcasted_iota(jnp.int32, (T, T), 1)
    earlier = jnp.where(row_t < col_t, 1.0, 0.0).astype(BF)
    before = dot(hit.astype(BF), earlier)
    chosen = jnp.where((before == place) & (hit > 0.5), 1.0, 0.0)
    sel = chosen.astype(BF)
    sel_tail = []

    def keep_weights(i, table):
        w = (weight * table).T
        w_hi = w.astype(BF)
        selw[2 * i] = w_hi
        selw[2 * i + 1] = (w - w_hi.astype(F32)).astype(BF)

    keep_weights(0, chosen)
    for g in range(groups):
        tail = jnp.where((place >= CAP) & (before == 3 * (place - CAP) + g) & (hit > 0.5), 1.0, 0.0)
        sel_tail.append(tail.astype(BF))
        keep_weights(1 + g, tail)
    slot_a = lax.broadcasted_iota(jnp.int32, (C, C), 0)
    slot_b = lax.broadcasted_iota(jnp.int32, (C, C), 1)

    def unpack(row, tail, g):
        at, to = lax.rem(row, SLOT), lax.rem(tail, SLOT)
        same = lax.div(row, SLOT) == lax.div(tail, SLOT)
        there = (to >= CAP) & (3 * (to - CAP) + g == at)
        return jnp.where(same & there, 1.0, 0.0).astype(BF)

    factor = math.log2(math.e) / math.sqrt(HD)
    W = min(256, LH * T)
    causal = jnp.concatenate([row_t <= col_t] * (W // T), axis=1)
    local[2].wait()
    for h in range(LH):
        q_t[:, h * T : (h + 1) * T] = q_v[:, h * HD : (h + 1) * HD].T

    def block(k_blk, v_blk, first):
        v_t = v_blk.T
        for w in range(LH * T // W):
            at = slice(w * W, (w + 1) * W)
            sc = dot(k_blk, q_t[:, at])
            if first:
                sc = jnp.where(causal, sc, masked_score)
                top = jnp.max(sc, axis=0, keepdims=True)
                pr = jnp.where(causal, jnp.exp2((sc - top) * factor), 0.0)
                l_s[:, at] = jnp.sum(pr, axis=0, keepdims=True)
                acc_s[:, at] = dot(v_t, pr.astype(BF))
            else:
                old = m_s[:, at]
                top = jnp.maximum(old, jnp.max(sc, axis=0, keepdims=True))
                pr = jnp.exp2((sc - top) * factor)
                keep = jnp.exp2((old - top) * factor)
                l_s[:, at] = l_s[:, at] * keep + jnp.sum(pr, axis=0, keepdims=True)
                acc_s[:, at] = acc_s[:, at] * keep + dot(v_t, pr.astype(BF))
            m_s[:, at] = top

    block(kv[c, :, :HD], kv[c, :, HD:], True)

    def kv_step(i):
        for o in (2 * i - 1, 2 * i):
            s = c - o
            @pl.when(s >= 0)
            def _():
                remote(half(s, p), half(s, p), kv_s.at[0], kv_r.at[s], c, sib).wait_recv()
                remote(half(s, p), half(s, p), kvf_s.at[s], kvf_r.at[s], c, sib).start()
        hi = c - (2 * i - 3)
        lo = hi - 1
        def arrived(s):
            remote(half(s, 1 - p), half(s, 1 - p), kvf_s.at[s], kvf_r.at[s], c, sib).wait_recv()
        @pl.when((i > 1) & (lo >= 0))
        def _():
            arrived(hi)
            arrived(lo)
            both = kv[pl.ds(lo, 2)].reshape(2 * T, 2 * HD)
            block(both[:, :HD], both[:, HD:], False)
        @pl.when((i > 1) & (lo == -1))
        def _():
            arrived(hi)
            block(kv[hi, :, :HD], kv[hi, :, HD:], False)
    loop(1, n // 2 + 2, kv_step)

    for copy in local[5:8]:
        copy.start()
    for h in range(LH):
        at = slice(h * T, (h + 1) * T)
        att[j, :, h * HD : (h + 1) * HD] = (acc_s[:, at] / l_s[:, at]).T.astype(BF)
    FC = F // AC

    def piece(jj, k):
        return att.at[jj, :, pl.ds(k * FC, FC)]

    for k in range(AC):
        for o in range(1, chips):
            t = other(o) * 2 + p
            remote(piece(j, k), piece(j, k), att_s.at[t, k], att_r.at[j, k], c, t).start()
        remote(piece(j, k), piece(j, k), att_s.at[sib, k], att_r.at[j, k], c, sib).start()

    local[3].wait()
    local[4].wait()

    def project(jj, k):
        return dot(att[jj, :, k * FC : (k + 1) * FC], wo[pl.ds(pl.multiple_of(jj * F + k * FC, FC), FC), :])

    out[...] = hid[...] + dot(att[j], wo[pl.ds(pl.multiple_of(j * F, F), F), :])
    for k in range(AC):
        remote(piece(sib, k), piece(sib, k), att_s.at[sib, k], att_r.at[sib, k], c, sib).wait_recv()
    if chips == 1:
        out[...] += dot(att[sib], wo[pl.ds(pl.multiple_of(sib * F, F), F), :])
    for o in range(1, chips):
        t = other(o) * 2 + p
        for k in range(AC):
            remote(piece(t, k), piece(t, k), att_s.at[t, k], att_r.at[t, k], c, sib).wait_recv()
            remote(piece(t, k), piece(t, k), attf_s.at[t, k], att_r.at[t, k], c, sib).start()
            if o == 1:
                out[...] += project(sib, k)
        out[...] += dot(att[t], wo[pl.ds(pl.multiple_of(t * F, F), F), :])
    for o in range(1, chips):
        t = other(o) * 2 + 1 - p
        for k in range(AC):
            remote(piece(t, k), piece(t, k), att_s.at[t, k], att_r.at[t, k], c, sib).wait_recv()
        out[...] += dot(att[t], wo[pl.ds(pl.multiple_of(t * F, F), F), :])

    mixed = out[...]
    xe[:, :F] = (mixed * gain[...]).astype(BF)
    squares = jnp.sum(mixed * mixed, axis=1, keepdims=True)
    part0 = squares.astype(BF).astype(F32)
    part1 = (squares - part0).astype(BF).astype(F32)
    part2 = squares - part0 - part1
    lane = lax.broadcasted_iota(jnp.int32, (T, EXTRA), 1)
    xe[:, F:] = jnp.where(
        lane == 0, part0, jnp.where(lane == 1, part1, jnp.where(lane == 2, part2, 0.0))
    ).astype(BF)
    outb[:, :, FP:] = dot(sel, xe[:, F:]).astype(BF).reshape(n, SLOT, EXTRA)
    if groups == 0:
        outb[:, :, :FP] = dot(sel, xe[:, :F]).astype(BF).reshape(n, SLOT, FP)
    for g in range(groups):
        at = slice(g * FQ, (g + 1) * FQ)
        got = dot(sel, xe[:, at]) + dot(sel_tail[g], xe[:, FP:F])
        outb[:, :, at] = got.astype(BF).reshape(n, SLOT, FQ)

    def d_send(o):
        d = lax.rem(c + o, n)
        remote(outb.at[d], arr.at[j, c], d_s.at[o], d_r.at[c], d, j).start()
    loop(1, n, d_send)
    arr[j, c] = outb[c]

    LAG = min(LAGS, NG - 1)
    own_group = lax.div(c, G)

    def rows(t, i):
        return arr.at[t, pl.ds(i * G, G)]

    def spread(i):
        for o in range(1, chips):
            t = other(o) * 2 + p
            remote(rows(j, i), rows(j, i), g_s.at[t, i], g_r.at[j, i], c, t).start()
        remote(rows(j, i), rows(j, i), g_s.at[sib, i], g_r.at[j, i], c, sib).start()

    def g_step(o):
        i = lax.rem(own_group + NG - o, NG)
        for o in range(1, chips):
            t = other(o) * 2 + p
            remote(rows(t, i), rows(t, i), g_s.at[t, i], g_r.at[t, i], c, sib).wait_recv()
            remote(rows(t, i), rows(t, i), gf_s.at[t, i], g_r.at[t, i], c, sib).start()

    def d_step(o):
        i = lax.rem(own_group + NG - o, NG)
        for k in range(G):
            s = i * G + k
            @pl.when(s != c)
            def _():
                remote(outb.at[s], arr.at[j, s], d_s.at[0], d_r.at[s], c, sib).wait_recv()
        spread(i)
        @pl.when(o >= LAG)
        def _():
            g_step(o - LAG)
    loop(0, NG, d_step)

    for i in range(5, 8):
        local[i].wait()

    def pre(t):
        x = arr[t].reshape(C, FP + EXTRA)
        at = pl.ds(pl.multiple_of(t * F, F), FP)
        sq = jnp.sum(x[:, FP:].astype(F32), axis=1, keepdims=True)
        gate, up = dot(x[:, :FP], wg[at, :]), dot(x[:, :FP], wu[at, :])
        if groups:
            tail = sum(dot(unpack(slot_a, slot_b, g), x[:, g * FQ : (g + 1) * FQ]) for g in range(groups)).astype(BF)
            at = pl.ds(pl.multiple_of(t * F + FP, FQ), FQ)
            gate, up = gate + dot(tail, wg[at, :]), up + dot(tail, wu[at, :])
        return gate, up, sq

    gate, up, sq = pre(j)

    def add(t, gate, up, sq):
        g1, u1, s1 = pre(t)
        return gate + g1, up + u1, sq + s1

    loop(NG - LAG, NG, g_step)

    def g_wait(t):
        def step(i):
            remote(rows(t, i), rows(t, i), g_s.at[t, i], g_r.at[t, i], c, sib).wait_recv()
        loop(0, NG, step)

    g_wait(sib)
    gate, up, sq = add(sib, gate, up, sq)
    for o in range(1, chips):
        gate, up, sq = add(other(o) * 2 + p, gate, up, sq)
    for o in range(1, chips):
        t = other(o) * 2 + 1 - p
        g_wait(t)
        gate, up, sq = add(t, gate, up, sq)
    used = lax.rem(lax.broadcasted_iota(jnp.int32, (C, 1), 0), SLOT) < CAP
    scale = jnp.where(used, lax.rsqrt(sq / D + epsilon), 0.0)
    gate = gate * scale
    up = up * scale
    act = (gate / (1.0 + jnp.exp(-gate)) * up).astype(BF)

    CR = C // NR
    NC = n // NR

    moved = [dot(unpack(slot_b, slot_a, g), act).astype(BF) for g in range(groups)]

    def down(t, r):
        rr = slice(r * CR, (r + 1) * CR)
        got = dot(act[rr], wd[:, pl.ds(pl.multiple_of(t * F, F), FP)])
        if groups:
            last = wd[:, pl.ds(pl.multiple_of(t * F + FP, FQ), FQ)]
            got = got + jnp.concatenate([dot(x[rr], last) for x in moved], axis=1)
        return got

    def at_rows(r):
        return pl.ds(r * CR, CR)

    def pair(r, q):
        return remote(pdown.at[q, at_rows(r)], pin.at[q, at_rows(r)], p_s.at[q, r], p_r.at[q, r], c, sib)

    def cross(r, o):
        q = other(o)
        return remote(xs.at[q, at_rows(r)], xin.at[chip, at_rows(r)], x_s.at[q, r], x_r.at[chip, r], c, q * 2 + p)

    for r in range(NR):
        for o in list(range(1, chips)) + [0]:
            q = other(o)
            pdown[q, r * CR : (r + 1) * CR] = down(q * 2 + 1 - p, r).astype(BF)
            pair(r, q).start()
    for r in range(NR):
        rr = slice(r * CR, (r + 1) * CR)
        for o in range(1, chips):
            q = other(o)
            part = down(q * 2 + p, r).astype(BF).astype(F32)
            pair(r, q).wait_recv()
            xs[q, rr] = (part + pin[q, rr].astype(F32)).astype(BF)
            cross(r, o).start()
    for r in range(NR):
        rr = slice(r * CR, (r + 1) * CR)
        mine[rr] = down(chip * 2 + p, r).astype(BF).astype(F32)
        pair(r, chip).wait_recv()
        mine[rr] += pin[chip, rr].astype(F32)
    for r in range(NR):
        rr = slice(r * CR, (r + 1) * CR)
        total = mine[rr]
        for o in range(1, chips):
            q = other(o)
            remote(xin.at[q, at_rows(r)], xin.at[q, at_rows(r)], x_s.at[q, r], x_r.at[q, r], c, sib).wait_recv()
            total = total + xin[q, rr].astype(F32)
        eo[r * NC : (r + 1) * NC] = total.astype(BF).reshape(NC, SLOT, FP)

        def r_send(s):
            @pl.when(s != c)
            def _():
                remote(eo.at[s], ret.at[c], r_s.at[s], r_r.at[c], s, j).start()
            @pl.when(s == c)
            def _():
                ret[c] = eo[c]
        loop(r * NC, (r + 1) * NC, r_send)

    def r_wait(s):
        @pl.when(s != c)
        def _():
            remote(eo.at[s], ret.at[s], r_s.at[s], r_r.at[s], s, j).wait_recv()
    loop(0, n, r_wait)
    back = ret[...].reshape(C, FP)
    out[:, :FP] += dot(selw[0], back) + dot(selw[1], back)
    for g in range(groups):
        piece_g = back[:, g * FQ : (g + 1) * FQ]
        out[:, FP:] += dot(selw[2 + 2 * g], piece_g) + dot(selw[3 + 2 * g], piece_g)

    kv_sent()
    att_sent()
    rows_sent()
    rest_sent()


def body(hidden, queries, keys, values, out_proj, gain, ids, weights, w_gate, w_up, w_down):
    n = lax.axis_size("ctx")
    m = lax.axis_size("et")
    T, F = hidden.shape
    U = w_gate.shape[2]
    LH = F // HD
    C = n * SLOT
    chips = m // 2
    AC = 4 if F % 512 == 0 else 2
    NR = 2
    G = 2
    LAGS = 7
    FP = F * CAP // SLOT if F % (128 * SLOT // (SLOT - CAP)) == 0 else F
    DMA = pltpu.SemaphoreType.DMA
    V = pltpu.VMEM
    any_ = pl.BlockSpec(memory_space=pl.ANY)
    vm = pl.BlockSpec(memory_space=pltpu.VMEM)
    return pl.pallas_call(
        functools.partial(kernel, n, m, AC, NR, G, LAGS),
        out_shape=jax.ShapeDtypeStruct((T, F), F32),
        in_specs=[any_, any_, any_, any_, any_, vm, vm, vm, any_, any_, any_],
        out_specs=vm,
        scratch_shapes=[
            V((T, F), BF),
            V((n, T, 2 * HD), BF),
            V((HD, LH * T), BF),
            V(out_proj.shape, BF),
            V(w_gate.shape[1:], BF),
            V(w_up.shape[1:], BF),
            V(w_down.shape[1:], BF),
            V((T, F), F32),
            V((1, LH * T), F32),
            V((1, LH * T), F32),
            V((HD, LH * T), F32),
            V((m, T, F), BF),
            V((T, F + EXTRA), BF),
            V((n, SLOT, FP + EXTRA), BF),
            V((m, n, SLOT, FP + EXTRA), BF),
            V((8, T, C), BF),
            V((chips, C, FP), BF),
            V((chips, C, FP), BF),
            V((C, FP), F32),
            V((chips, C, FP), BF),
            V((chips, C, FP), BF),
            V((n, SLOT, FP), BF),
            V((n, SLOT, FP), BF),
            DMA((8,)),
            DMA((n,)), DMA((n,)), DMA((n,)), DMA((n,)),
            DMA((m, AC)), DMA((m, AC)), DMA((m, AC)),
            DMA((n,)), DMA((n,)),
            DMA((m, n // G)), DMA((m, n // G)), DMA((m, n // G)),
            DMA((chips, NR)), DMA((chips, NR)),
            DMA((chips, NR)), DMA((chips, NR)),
            DMA((n,)), DMA((n,)),
        ],
        compiler_params=pltpu.CompilerParams(
            collective_id=0, has_side_effects=True, vmem_limit_bytes=58 * 1024 * 1024
        ),
        cost_estimate=pl.CostEstimate(flops=4 * 10**9, bytes_accessed=2 * 10**7, transcendentals=10**6),
    )(
        hidden, queries, keys, values, out_proj, gain.reshape(1, F), ids.T, weights.T,
        w_gate, w_up, w_down,
    )


def solution(mesh):
    return jax.shard_map(
        body,
        mesh=mesh,
        in_specs=(
            P("ctx", "et"),
            P("ctx", "et"),
            P("ctx", None),
            P("ctx", None),
            P(None, "et"),
            P("et"),
            P("ctx", None),
            P("ctx", None),
            P("ctx", None, "et"),
            P("ctx", None, "et"),
            P("ctx", "et", None),
        ),
        out_specs=P("ctx", "et"),
        check_vma=False,
    )
```

```python
import functools
import math

import jax
import jax.numpy as jnp
from jax import lax
from jax.experimental import pallas as pl
from jax.experimental.pallas import tpu as pltpu
from jax.sharding import PartitionSpec as P

D = 4096
HEADS = 32
KV_HEADS = 2
HD = 128
CAP = 12
SLOT = 16
EXTRA = 128

epsilon = 1e-06
masked_score = -1e30
BF = jnp.bfloat16
F32 = jnp.float32


def dot(a, b):
    return jnp.dot(a, b, preferred_element_type=F32)


def kernel(
    n, m, AC, NR, G, LAGS,
    hidden, queries, keys, values, out_proj, gain, ids, weights, w_gate, w_up, w_down,
    out,
    q_v, kv, q_t, wo, wg, wu, wd, hid,
    m_s, l_s, acc_s, att, xe, outb, arr, selw, pdown, pin, mine, xs, xin, eo, ret,
    lsem, kv_s, kv_r, kvf_s, kvf_r, att_s, att_r, attf_s,
    d_s, d_r, g_s, g_r, gf_s, p_s, p_r, x_s, x_r, r_s, r_r,
):
    T, F = hidden.shape
    LH = F // HD
    group = HEADS // KV_HEADS
    C = n * SLOT
    U = w_gate.shape[2]
    chips = m // 2
    NG = n // G
    FP = arr.shape[3] - EXTRA
    FQ = F - FP
    groups = FP // FQ if FQ else 0
    c = lax.axis_index("ctx")
    j = lax.axis_index("et")
    p = lax.rem(j, 2)
    chip = lax.div(j, 2)
    sib = j + 1 - 2 * p
    kvh = lax.div(j * LH, group)
    head_lanes = pl.ds(pl.multiple_of(kvh * HD, HD), HD)

    def other(o):
        return lax.rem(chip + o, chips)

    def remote(src, dst, ssem, rsem, dc, dj):
        return pltpu.make_async_remote_copy(
            src_ref=src, dst_ref=dst, send_sem=ssem, recv_sem=rsem,
            device_id=(dc, dj), device_id_type=pl.DeviceIdType.MESH,
        )

    def loop(lo, hi, f):
        def step(i, carry):
            f(i)
            return carry
        lax.fori_loop(lo, hi, step, 0)

    def kv_sent():
        def step(o):
            @pl.when(c + o < n)
            def _():
                remote(half(c, p), half(c, p), kv_s.at[o], kv_r.at[c], c, sib).wait_send()
            @pl.when(c - o >= 0)
            def _():
                s = c - o
                remote(half(s, p), half(s, p), kvf_s.at[s], kvf_r.at[s], c, sib).wait_send()
        loop(1, n, step)

    def att_sent():
        for k in range(AC):
            for o in range(1, chips):
                t = other(o) * 2 + p
                remote(piece(j, k), piece(j, k), att_s.at[t, k], att_r.at[j, k], c, t).wait_send()
                remote(piece(t, k), piece(t, k), attf_s.at[t, k], att_r.at[t, k], c, sib).wait_send()
            remote(piece(j, k), piece(j, k), att_s.at[sib, k], att_r.at[j, k], c, sib).wait_send()

    def rows_sent():
        def step(s):
            remote(outb.at[s], arr.at[j, c], d_s.at[s], d_r.at[c], c, sib).wait_send()
        loop(1, n, step)

        def step_group(i):
            for o in range(1, chips):
                t = other(o) * 2 + p
                remote(rows(j, i), rows(j, i), g_s.at[t, i], g_r.at[j, i], c, t).wait_send()
                remote(rows(t, i), rows(t, i), gf_s.at[t, i], g_r.at[t, i], c, sib).wait_send()
            remote(rows(j, i), rows(j, i), g_s.at[sib, i], g_r.at[j, i], c, sib).wait_send()
        loop(0, NG, step_group)

    def rest_sent():
        for r in range(NR):
            for o in range(chips):
                pair(r, other(o)).wait_send()
            for o in range(1, chips):
                cross(r, o).wait_send()
        def step(s):
            @pl.when(s != c)
            def _():
                remote(eo.at[s], ret.at[c], r_s.at[s], r_r.at[c], s, j).wait_send()
        loop(0, n, step)

    local = [
        pltpu.make_async_copy(keys.at[:, head_lanes], kv.at[c, :, pl.ds(0, HD)], lsem.at[0]),
        pltpu.make_async_copy(values.at[:, head_lanes], kv.at[c, :, pl.ds(HD, HD)], lsem.at[1]),
        pltpu.make_async_copy(queries, q_v, lsem.at[2]),
        pltpu.make_async_copy(hidden, hid, lsem.at[3]),
        pltpu.make_async_copy(out_proj, wo, lsem.at[4]),
        pltpu.make_async_copy(w_gate.at[0], wg, lsem.at[5]),
        pltpu.make_async_copy(w_up.at[0], wu, lsem.at[6]),
        pltpu.make_async_copy(w_down.at[0], wd, lsem.at[7]),
    ]
    for copy in local[:3]:
        copy.start()

    barrier = pltpu.get_barrier_semaphore()
    for o in range(1, n):
        pl.semaphore_signal(barrier, inc=1, device_id=(lax.rem(c + o, n), j), device_id_type=pl.DeviceIdType.MESH)
    for o in range(1, m):
        pl.semaphore_signal(barrier, inc=1, device_id=(c, lax.rem(j + o, m)), device_id_type=pl.DeviceIdType.MESH)
    local[0].wait()
    local[1].wait()
    pl.semaphore_wait(barrier, n - 1 + m - 1)

    def half(s, which):
        return kv.at[s, :, pl.ds(pl.multiple_of(which * HD, HD), HD)]

    def kv_send(o):
        d = c + o
        @pl.when(d < n)
        def _():
            remote(half(c, p), half(c, p), kv_s.at[o], kv_r.at[c], d, j).start()
    loop(1, n, kv_send)
    for copy in local[3:5]:
        copy.start()

    slot_row = lax.broadcasted_iota(jnp.int32, (C, T), 0)
    expert_row = lax.div(slot_row, SLOT)
    place = lax.rem(slot_row, SLOT).astype(F32)
    hit = jnp.zeros((C, T), F32)
    weight = jnp.zeros((C, T), F32)
    for k in range(ids.shape[0]):
        same = ids[k : k + 1, :] == expert_row
        hit = hit + jnp.where(same, 1.0, 0.0)
        weight = weight + jnp.where(same, weights[k : k + 1, :], 0.0)
    row_t = lax.broadcasted_iota(jnp.int32, (T, T), 0)
    col_t = lax.broadcasted_iota(jnp.int32, (T, T), 1)
    earlier = jnp.where(row_t < col_t, 1.0, 0.0).astype(BF)
    before = dot(hit.astype(BF), earlier)
    chosen = jnp.where((before == place) & (hit > 0.5), 1.0, 0.0)
    sel = chosen.astype(BF)
    sel_tail = []

    def keep_weights(i, table):
        w = (weight * table).T
        w_hi = w.astype(BF)
        selw[2 * i] = w_hi
        selw[2 * i + 1] = (w - w_hi.astype(F32)).astype(BF)

    keep_weights(0, chosen)
    for g in range(groups):
        tail = jnp.where((place >= CAP) & (before == 3 * (place - CAP) + g) & (hit > 0.5), 1.0, 0.0)
        sel_tail.append(tail.astype(BF))
        keep_weights(1 + g, tail)
    slot_a = lax.broadcasted_iota(jnp.int32, (C, C), 0)
    slot_b = lax.broadcasted_iota(jnp.int32, (C, C), 1)

    def unpack(row, tail, g):
        at, to = lax.rem(row, SLOT), lax.rem(tail, SLOT)
        same = lax.div(row, SLOT) == lax.div(tail, SLOT)
        there = (to >= CAP) & (3 * (to - CAP) + g == at)
        return jnp.where(same & there, 1.0, 0.0).astype(BF)

    factor = math.log2(math.e) / math.sqrt(HD)
    W = min(256, LH * T)
    causal = jnp.concatenate([row_t <= col_t] * (W // T), axis=1)
    local[2].wait()
    for h in range(LH):
        q_t[:, h * T : (h + 1) * T] = q_v[:, h * HD : (h + 1) * HD].T

    def block(k_blk, v_blk, first):
        v_t = v_blk.T
        for w in range(LH * T // W):
            at = slice(w * W, (w + 1) * W)
            sc = dot(k_blk, q_t[:, at])
            if first:
                sc = jnp.where(causal, sc, masked_score)
                top = jnp.max(sc, axis=0, keepdims=True)
                pr = jnp.where(causal, jnp.exp2((sc - top) * factor), 0.0)
                l_s[:, at] = jnp.sum(pr, axis=0, keepdims=True)
                acc_s[:, at] = dot(v_t, pr.astype(BF))
            else:
                old = m_s[:, at]
                top = jnp.maximum(old, jnp.max(sc, axis=0, keepdims=True))
                pr = jnp.exp2((sc - top) * factor)
                keep = jnp.exp2((old - top) * factor)
                l_s[:, at] = l_s[:, at] * keep + jnp.sum(pr, axis=0, keepdims=True)
                acc_s[:, at] = acc_s[:, at] * keep + dot(v_t, pr.astype(BF))
            m_s[:, at] = top

    block(kv[c, :, :HD], kv[c, :, HD:], True)

    def kv_step(i):
        for o in (2 * i - 1, 2 * i):
            s = c - o
            @pl.when(s >= 0)
            def _():
                remote(half(s, p), half(s, p), kv_s.at[0], kv_r.at[s], c, sib).wait_recv()
                remote(half(s, p), half(s, p), kvf_s.at[s], kvf_r.at[s], c, sib).start()
        hi = c - (2 * i - 3)
        lo = hi - 1
        def arrived(s):
            remote(half(s, 1 - p), half(s, 1 - p), kvf_s.at[s], kvf_r.at[s], c, sib).wait_recv()
        @pl.when((i > 1) & (lo >= 0))
        def _():
            arrived(hi)
            arrived(lo)
            both = kv[pl.ds(lo, 2)].reshape(2 * T, 2 * HD)
            block(both[:, :HD], both[:, HD:], False)
        @pl.when((i > 1) & (lo == -1))
        def _():
            arrived(hi)
            block(kv[hi, :, :HD], kv[hi, :, HD:], False)
    loop(1, n // 2 + 2, kv_step)

    for copy in local[5:8]:
        copy.start()
    for h in range(LH):
        at = slice(h * T, (h + 1) * T)
        att[j, :, h * HD : (h + 1) * HD] = (acc_s[:, at] / l_s[:, at]).T.astype(BF)
    FC = F // AC

    def piece(jj, k):
        return att.at[jj, :, pl.ds(k * FC, FC)]

    for k in range(AC):
        for o in range(1, chips):
            t = other(o) * 2 + p
            remote(piece(j, k), piece(j, k), att_s.at[t, k], att_r.at[j, k], c, t).start()
        remote(piece(j, k), piece(j, k), att_s.at[sib, k], att_r.at[j, k], c, sib).start()

    local[3].wait()
    local[4].wait()

    def project(jj, k):
        return dot(att[jj, :, k * FC : (k + 1) * FC], wo[pl.ds(pl.multiple_of(jj * F + k * FC, FC), FC), :])

    out[...] = hid[...] + dot(att[j], wo[pl.ds(pl.multiple_of(j * F, F), F), :])
    for k in range(AC):
        remote(piece(sib, k), piece(sib, k), att_s.at[sib, k], att_r.at[sib, k], c, sib).wait_recv()
    if chips == 1:
        out[...] += dot(att[sib], wo[pl.ds(pl.multiple_of(sib * F, F), F), :])
    for o in range(1, chips):
        t = other(o) * 2 + p
        for k in range(AC):
            remote(piece(t, k), piece(t, k), att_s.at[t, k], att_r.at[t, k], c, sib).wait_recv()
            remote(piece(t, k), piece(t, k), attf_s.at[t, k], att_r.at[t, k], c, sib).start()
            if o == 1:
                out[...] += project(sib, k)
        out[...] += dot(att[t], wo[pl.ds(pl.multiple_of(t * F, F), F), :])
    for o in range(1, chips):
        t = other(o) * 2 + 1 - p
        for k in range(AC):
            remote(piece(t, k), piece(t, k), att_s.at[t, k], att_r.at[t, k], c, sib).wait_recv()
        out[...] += dot(att[t], wo[pl.ds(pl.multiple_of(t * F, F), F), :])

    mixed = out[...]
    xe[:, :F] = (mixed * gain[...]).astype(BF)
    squares = jnp.sum(mixed * mixed, axis=1, keepdims=True)
    part0 = squares.astype(BF).astype(F32)
    part1 = (squares - part0).astype(BF).astype(F32)
    part2 = squares - part0 - part1
    lane = lax.broadcasted_iota(jnp.int32, (T, EXTRA), 1)
    xe[:, F:] = jnp.where(
        lane == 0, part0, jnp.where(lane == 1, part1, jnp.where(lane == 2, part2, 0.0))
    ).astype(BF)
    outb[:, :, FP:] = dot(sel, xe[:, F:]).astype(BF).reshape(n, SLOT, EXTRA)
    if groups == 0:
        outb[:, :, :FP] = dot(sel, xe[:, :F]).astype(BF).reshape(n, SLOT, FP)
    for g in range(groups):
        at = slice(g * FQ, (g + 1) * FQ)
        got = dot(sel, xe[:, at]) + dot(sel_tail[g], xe[:, FP:F])
        outb[:, :, at] = got.astype(BF).reshape(n, SLOT, FQ)

    def d_send(o):
        d = lax.rem(c + o, n)
        remote(outb.at[d], arr.at[j, c], d_s.at[o], d_r.at[c], d, j).start()
    loop(1, n, d_send)
    arr[j, c] = outb[c]

    LAG = min(LAGS, NG - 1)
    own_group = lax.div(c, G)

    def rows(t, i):
        return arr.at[t, pl.ds(i * G, G)]

    def spread(i):
        for o in range(1, chips):
            t = other(o) * 2 + p
            remote(rows(j, i), rows(j, i), g_s.at[t, i], g_r.at[j, i], c, t).start()
        remote(rows(j, i), rows(j, i), g_s.at[sib, i], g_r.at[j, i], c, sib).start()

    def g_step(o):
        i = lax.rem(own_group + NG - o, NG)
        for o in range(1, chips):
            t = other(o) * 2 + p
            remote(rows(t, i), rows(t, i), g_s.at[t, i], g_r.at[t, i], c, sib).wait_recv()
            remote(rows(t, i), rows(t, i), gf_s.at[t, i], g_r.at[t, i], c, sib).start()

    def d_step(o):
        i = lax.rem(own_group + NG - o, NG)
        for k in range(G):
            s = i * G + k
            @pl.when(s != c)
            def _():
                remote(outb.at[s], arr.at[j, s], d_s.at[0], d_r.at[s], c, sib).wait_recv()
        spread(i)
        @pl.when(o >= LAG)
        def _():
            g_step(o - LAG)
    loop(0, NG, d_step)

    for i in range(5, 8):
        local[i].wait()

    def pre(t):
        x = arr[t].reshape(C, FP + EXTRA)
        at = pl.ds(pl.multiple_of(t * F, F), FP)
        sq = jnp.sum(x[:, FP:].astype(F32), axis=1, keepdims=True)
        gate, up = dot(x[:, :FP], wg[at, :]), dot(x[:, :FP], wu[at, :])
        if groups:
            tail = sum(dot(unpack(slot_a, slot_b, g), x[:, g * FQ : (g + 1) * FQ]) for g in range(groups)).astype(BF)
            at = pl.ds(pl.multiple_of(t * F + FP, FQ), FQ)
            gate, up = gate + dot(tail, wg[at, :]), up + dot(tail, wu[at, :])
        return gate, up, sq

    gate, up, sq = pre(j)

    def add(t, gate, up, sq):
        g1, u1, s1 = pre(t)
        return gate + g1, up + u1, sq + s1

    loop(NG - LAG, NG, g_step)

    def g_wait(t):
        def step(i):
            remote(rows(t, i), rows(t, i), g_s.at[t, i], g_r.at[t, i], c, sib).wait_recv()
        loop(0, NG, step)

    g_wait(sib)
    gate, up, sq = add(sib, gate, up, sq)
    for o in range(1, chips):
        gate, up, sq = add(other(o) * 2 + p, gate, up, sq)
    for o in range(1, chips):
        t = other(o) * 2 + 1 - p
        g_wait(t)
        gate, up, sq = add(t, gate, up, sq)
    used = lax.rem(lax.broadcasted_iota(jnp.int32, (C, 1), 0), SLOT) < CAP
    scale = jnp.where(used, lax.rsqrt(sq / D + epsilon), 0.0)
    gate = gate * scale
    up = up * scale
    act = (gate / (1.0 + jnp.exp(-gate)) * up).astype(BF)

    CR = C // NR
    NC = n // NR

    moved = [dot(unpack(slot_b, slot_a, g), act).astype(BF) for g in range(groups)]

    def down(t, r):
        rr = slice(r * CR, (r + 1) * CR)
        got = dot(act[rr], wd[:, pl.ds(pl.multiple_of(t * F, F), FP)])
        if groups:
            last = wd[:, pl.ds(pl.multiple_of(t * F + FP, FQ), FQ)]
            got = got + jnp.concatenate([dot(x[rr], last) for x in moved], axis=1)
        return got

    def at_rows(r):
        return pl.ds(r * CR, CR)

    def pair(r, q):
        return remote(pdown.at[q, at_rows(r)], pin.at[q, at_rows(r)], p_s.at[q, r], p_r.at[q, r], c, sib)

    def cross(r, o):
        q = other(o)
        return remote(xs.at[q, at_rows(r)], xin.at[chip, at_rows(r)], x_s.at[q, r], x_r.at[chip, r], c, q * 2 + p)

    for r in range(NR):
        for o in range(1, chips):
            q = other(o)
            pdown[q, r * CR : (r + 1) * CR] = down(q * 2 + 1 - p, r).astype(BF)
            pair(r, q).start()
    for r in range(NR):
        rr = slice(r * CR, (r + 1) * CR)
        for o in range(1, chips):
            q = other(o)
            part = down(q * 2 + p, r).astype(BF).astype(F32)
            pair(r, q).wait_recv()
            xs[q, rr] = (part + pin[q, rr].astype(F32)).astype(BF)
            cross(r, o).start()
    for r in range(NR):
        for o in [0]:
            q = other(o)
            pdown[q, r * CR : (r + 1) * CR] = down(q * 2 + 1 - p, r).astype(BF)
            pair(r, q).start()
    for r in range(NR):
        rr = slice(r * CR, (r + 1) * CR)
        mine[rr] = down(chip * 2 + p, r).astype(BF).astype(F32)
        pair(r, chip).wait_recv()
        mine[rr] += pin[chip, rr].astype(F32)
    for r in range(NR):
        rr = slice(r * CR, (r + 1) * CR)
        total = mine[rr]
        for o in range(1, chips):
            q = other(o)
            remote(xin.at[q, at_rows(r)], xin.at[q, at_rows(r)], x_s.at[q, r], x_r.at[q, r], c, sib).wait_recv()
            total = total + xin[q, rr].astype(F32)
        eo[r * NC : (r + 1) * NC] = total.astype(BF).reshape(NC, SLOT, FP)

        def r_send(s):
            @pl.when(s != c)
            def _():
                remote(eo.at[s], ret.at[c], r_s.at[s], r_r.at[c], s, j).start()
            @pl.when(s == c)
            def _():
                ret[c] = eo[c]
        loop(r * NC, (r + 1) * NC, r_send)

    def r_wait(s):
        @pl.when(s != c)
        def _():
            remote(eo.at[s], ret.at[s], r_s.at[s], r_r.at[s], s, j).wait_recv()
    loop(0, n, r_wait)
    back = ret[...].reshape(C, FP)
    out[:, :FP] += dot(selw[0], back) + dot(selw[1], back)
    for g in range(groups):
        piece_g = back[:, g * FQ : (g + 1) * FQ]
        out[:, FP:] += dot(selw[2 + 2 * g], piece_g) + dot(selw[3 + 2 * g], piece_g)

    kv_sent()
    att_sent()
    rows_sent()
    rest_sent()


def body(hidden, queries, keys, values, out_proj, gain, ids, weights, w_gate, w_up, w_down):
    n = lax.axis_size("ctx")
    m = lax.axis_size("et")
    T, F = hidden.shape
    U = w_gate.shape[2]
    LH = F // HD
    C = n * SLOT
    chips = m // 2
    AC = 4 if F % 512 == 0 else 2
    NR = 2
    G = 2
    LAGS = 7
    FP = F * CAP // SLOT if F % (128 * SLOT // (SLOT - CAP)) == 0 else F
    DMA = pltpu.SemaphoreType.DMA
    V = pltpu.VMEM
    any_ = pl.BlockSpec(memory_space=pl.ANY)
    vm = pl.BlockSpec(memory_space=pltpu.VMEM)
    return pl.pallas_call(
        functools.partial(kernel, n, m, AC, NR, G, LAGS),
        out_shape=jax.ShapeDtypeStruct((T, F), F32),
        in_specs=[any_, any_, any_, any_, any_, vm, vm, vm, any_, any_, any_],
        out_specs=vm,
        scratch_shapes=[
            V((T, F), BF),
            V((n, T, 2 * HD), BF),
            V((HD, LH * T), BF),
            V(out_proj.shape, BF),
            V(w_gate.shape[1:], BF),
            V(w_up.shape[1:], BF),
            V(w_down.shape[1:], BF),
            V((T, F), F32),
            V((1, LH * T), F32),
            V((1, LH * T), F32),
            V((HD, LH * T), F32),
            V((m, T, F), BF),
            V((T, F + EXTRA), BF),
            V((n, SLOT, FP + EXTRA), BF),
            V((m, n, SLOT, FP + EXTRA), BF),
            V((8, T, C), BF),
            V((chips, C, FP), BF),
            V((chips, C, FP), BF),
            V((C, FP), F32),
            V((chips, C, FP), BF),
            V((chips, C, FP), BF),
            V((n, SLOT, FP), BF),
            V((n, SLOT, FP), BF),
            DMA((8,)),
            DMA((n,)), DMA((n,)), DMA((n,)), DMA((n,)),
            DMA((m, AC)), DMA((m, AC)), DMA((m, AC)),
            DMA((n,)), DMA((n,)),
            DMA((m, n // G)), DMA((m, n // G)), DMA((m, n // G)),
            DMA((chips, NR)), DMA((chips, NR)),
            DMA((chips, NR)), DMA((chips, NR)),
            DMA((n,)), DMA((n,)),
        ],
        compiler_params=pltpu.CompilerParams(
            collective_id=0, has_side_effects=True, vmem_limit_bytes=58 * 1024 * 1024
        ),
        cost_estimate=pl.CostEstimate(flops=4 * 10**9, bytes_accessed=2 * 10**7, transcendentals=10**6),
    )(
        hidden, queries, keys, values, out_proj, gain.reshape(1, F), ids.T, weights.T,
        w_gate, w_up, w_down,
    )


def solution(mesh):
    return jax.shard_map(
        body,
        mesh=mesh,
        in_specs=(
            P("ctx", "et"),
            P("ctx", "et"),
            P("ctx", None),
            P("ctx", None),
            P(None, "et"),
            P("et"),
            P("ctx", None),
            P("ctx", None),
            P("ctx", None, "et"),
            P("ctx", None, "et"),
            P("ctx", "et", None),
        ),
        out_specs=P("ctx", "et"),
        check_vma=False,
    )
```
